32 devices in a mesh: groups: 2 (over x), vocab: 16 (over z, y, core).
Axes of the slice: x: 2, y: 2, z: 4, core: 2. Of those that a mesh axis runs over, the one named last changes fastest.
Arguments:
- hidden: bfloat16 [256, 8192], P('groups'), parts along dimension 0, may hold values from -312 to 312
- student_weight: bfloat16 [8192, 8192], P(None, 'vocab'), may hold values from -0.0625 to 0.0625
- teacher_codes: bfloat16 [16384, 256], P('vocab', 'groups'), parts along dimension 1, may hold values from -12 to 120
- teacher_exps: int32 [512, 256], P('vocab', 'groups'), parts along dimension 1, may hold values from -2 to 1
- pair_tile: int32 [384], P('vocab'), may hold values from 0 to 7
- pair_dest: int32 [384, 1], P('vocab'), may hold values from 0 to 15; in each aligned block of 24 rows (0 to 23, 24 to 47, ...) at most 2 rows name the same one
- pair_block: int32 [384], P('vocab'), may hold values from 0 to 3
- pair_map: int32 [384, 128], P('vocab'), may hold values from 0 to 159
Outputs:
- grad_hidden: bfloat16 [8192, 256], P('vocab', 'groups'), parts along dimension 1
The draws below stay inside these ranges and needn't reach their ends.
There are 2 independent parts, one for each index of `groups`. The reference program is written for one: setup_inputs(seed, part) draws one part's arguments, and reference() takes and returns one part's arrays. A program takes and returns all parts, laid end to end along the dimension named above; an argument that names none is the same for every part. Nothing has to cross between parts.
Inputs may be any that keep to these rules, and one draw needn't show every extreme that they name: `pair_dest`: each aligned block of 24 rows is one vocab index's list; in it no owner is named more than 2 times, a bound that some block reaches. `pair_map`: entries of 128 or more join the teacher entry to no student entry.
All inputs are finite; a program needn't handle non-finite values.
Results may differ from the reference program's by a relative error of at most 0.001.
The reference program's roundings to bfloat16 on the way (of `teacher_probs` and `residual`) count: a program that leaves them out, or rounds other values in their place, can miss the bound.
Values may be sent and summed in bfloat16 or wider, within the bound.
A program may use at most 128 MiB of HBM per device.

```python
import math
import jax
import jax.numpy as jnp
import numpy as np
from jax import lax

D = 8192
V_DEV = 512
BLK = 128
CAP = 2
TOK = 128
OWNERS = 16
PAIRS_DEV = 24
SB_DEV = 4
TB_DEV = 8
VS = 8192
TV = 16384
PAIRS = 384


def draw_hidden(key, part):
    key = jax.random.fold_in(key, 11)
    value_key = jax.random.fold_in(key, 0)
    values = 3.0 * jax.random.truncated_normal(value_key, -4.0, 4.0, (TOK, D), jnp.float32)
    return values.astype(jnp.bfloat16)


def draw_teacher_codes(key, part):
    key = jax.random.fold_in(key, 23)
    value_key = jax.random.fold_in(key, 0)
    values = 3.0 * jax.random.truncated_normal(value_key, -4.0, 4.0, (TV, TOK), jnp.float32)
    return values.astype(jnp.bfloat16)


def with_ends(array, own_key, low, top_value):
    place = [jax.random.randint(jax.random.fold_in(own_key, axis), (), 0, length) for axis, length in enumerate(array.shape)]
    widest = array.shape.index(max(array.shape))
    next_to = place[:widest] + [(place[widest] + 1) % array.shape[widest]] + place[widest + 1:]
    return array.at[tuple(place)].set(low).at[tuple(next_to)].set(top_value)


def level_of(stream_key, dims, shards, least, top_value):
    def one(dim, shards_of):
        draws = jax.random.uniform(jax.random.fold_in(jax.random.fold_in(stream_key, 6), dim), (shards_of,), jnp.float32, least / len(shards), top_value / len(shards))
        return jnp.repeat(jnp.exp(draws), dims[dim] // shards_of).reshape((-1,) + (1,) * (len(dims) - dim - 1))

    level = one(*shards[0])
    for cut in shards[1:]:
        level = level * one(*cut)
    return level


def shared_out(key, own, number, rows, amount, top, limit, slope):
    order = jax.random.permutation(key, amount)
    crowded, ordinary = load_shares(amount, rows * top, limit, slope, True), load_shares(amount, rows * top, limit, slope, False)
    places = jnp.arange(amount)

    def named(sizes, offset_by):
        used = int((sizes > 0).sum())
        fixed = max(1, used // 4)
        passed = fixed + (places - fixed + offset_by * (used - fixed)) % max(1, amount - fixed)
        return jnp.zeros((amount,), jnp.int32).at[order[jnp.where(places < fixed, places, passed)]].set(jnp.asarray(sizes, jnp.int32))

    sizes = jnp.where(number % 4 == 0, named(crowded, number // 4), named(ordinary, number - number // 4 - 1))
    mixed = jax.random.permutation(jax.random.fold_in(own, 3), amount)
    source_of, receiver = mixed[0:amount // 2 * 2:2], mixed[1:amount // 2 * 2:2]
    margin = jnp.minimum(sizes[source_of] - 1, limit - sizes[receiver]) // 2
    margin = jnp.where((source_of == order[0]) | (receiver == order[0]) | (sizes[receiver] == 0), 0, jnp.maximum(margin, 0))
    passed = jax.random.randint(jax.random.fold_in(own, 4), (amount // 2,), 0, 1 << 20) % (margin + 1)
    sizes = sizes.at[source_of].add(-passed).at[receiver].add(passed)
    members = jnp.searchsorted(jnp.cumsum(sizes), jnp.arange(rows * top), side="right").astype(jnp.int32)
    grid = members.reshape(top, rows).T
    grid = grid[jax.random.permutation(jax.random.fold_in(own, 1), rows)]
    offset_by = jax.random.randint(jax.random.fold_in(own, 2), (rows, 1), 0, top)
    return jnp.take_along_axis(grid, (jnp.arange(top)[None, :] + offset_by) % top, axis=1)


def load_shares(number_of, total, limit, skew, full):
    portions = [(1 << 20) // math.isqrt(grade ** skew) + 1 for grade in range(1, number_of + 1)]
    largest = limit if full else min(limit, max(-(-total // number_of), total * portions[0] // sum(portions)))
    least = 1 if total - largest >= number_of - 1 else 0
    given, rest = [largest] + [least] * (number_of - 1), total - largest - least * (number_of - 1)
    while rest > 0:
        candidates = [i for i in range(1, number_of) if given[i] < largest] or [i for i in range(1, number_of) if given[i] < limit]
        mass, budget = sum([portions[i] for i in candidates]), rest
        for i in candidates:
            addition = min(limit - given[i], max(1, budget * portions[i] // mass), rest)
            given[i] = given[i] + addition
            rest = rest - addition
    return np.array(given)


def noise(stream_key, dims, scale, bound, cuts=(), kind=jnp.bfloat16):
    entries = jax.random.normal(stream_key, dims, jnp.float32) * scale
    if len(cuts) > 0:
        entries = level_of(stream_key, dims, cuts, -0.22, 0.18) * entries
    return jnp.clip(entries, min=-bound, max=bound).astype(kind)


def setup_inputs(seed: int = 0, part: int = 0) -> dict:
    seeds = jax.random.split(jax.random.key(seed), 9)
    part_keys = jax.random.split(jax.random.fold_in(seeds[8], part), 9)
    hidden = draw_hidden(jax.random.fold_in(jax.random.fold_in(seeds[8], part), 71), part)
    student_weight = noise(seeds[1], (D, VS), D ** -0.5, 0.0625, ((1, 16),))
    teacher_codes = draw_teacher_codes(jax.random.fold_in(jax.random.fold_in(seeds[8], part), 71), part)
    teacher_exps = with_ends(jax.random.randint(part_keys[3], (TV // 32, TOK), -2, 2), jax.random.fold_in(part_keys[3], 1), -2, 1).astype(jnp.int32)
    pair_tile = with_ends(jax.random.randint(seeds[4], (PAIRS,), 0, TB_DEV), jax.random.fold_in(seeds[4], 1), 0, TB_DEV - 1).astype(jnp.int32)
    pair_dest_keys = jax.random.split(jax.random.fold_in(seeds[5], 1), PAIRS // PAIRS_DEV)
    pair_dest_turns = jax.random.permutation(jax.random.fold_in(seeds[5], 3), PAIRS // PAIRS_DEV)
    pair_dest = jax.vmap(lambda own, number: shared_out(jax.random.fold_in(seeds[5], 2), own, number, PAIRS_DEV, OWNERS, 1, CAP, 2))(pair_dest_keys, pair_dest_turns).reshape((PAIRS, 1))
    pair_block = with_ends(jax.random.randint(seeds[6], (PAIRS,), 0, SB_DEV), jax.random.fold_in(seeds[6], 1), 0, SB_DEV - 1).astype(jnp.int32)
    pair_map = with_ends(jax.random.randint(seeds[7], (PAIRS, BLK), 0, BLK + BLK // 4), jax.random.fold_in(seeds[7], 1), 0, (BLK + BLK // 4) - 1).astype(jnp.int32)
    return {"hidden": hidden, "student_weight": student_weight, "teacher_codes": teacher_codes, "teacher_exps": teacher_exps, "pair_tile": pair_tile, "pair_dest": pair_dest, "pair_block": pair_block, "pair_map": pair_map}


smoothing = 0.05
loss_scale = 64.0


def log_normalizer(values):
    maximum = jnp.max(values, axis=0)
    return maximum + jnp.log(jnp.sum(jnp.exp(values - maximum[None, :]), axis=0))


def reference(hidden, student_weight, teacher_codes, teacher_exps, pair_tile, pair_dest, pair_block, pair_map):
    scales = jnp.exp2(jnp.repeat(teacher_exps.astype(jnp.float32), 32, axis=0))
    teacher_logits = teacher_codes.astype(jnp.float32) * scales
    teacher_lse = log_normalizer(teacher_logits)
    teacher_probs = jnp.exp(teacher_logits - teacher_lse[None, :]).astype(jnp.bfloat16)
    offsets = jnp.arange(BLK, dtype=jnp.int32)

    def add_owner(owner_index, mapped):
        owner_index = owner_index.astype(jnp.int32)
        first_row = (owner_index * PAIRS_DEV).astype(jnp.int32)
        tile_ids = lax.dynamic_slice_in_dim(pair_tile, first_row, PAIRS_DEV, 0)
        targets = lax.dynamic_slice_in_dim(pair_dest[:, 0], first_row, PAIRS_DEV, 0)
        blocks = lax.dynamic_slice_in_dim(pair_block, first_row, PAIRS_DEV, 0)
        map_rows = lax.dynamic_slice_in_dim(pair_map, first_row, PAIRS_DEV, 0)
        row_ids = ((owner_index * TB_DEV + tile_ids) * BLK)[:, None] + offsets[None, :]
        columns = (targets * V_DEV + blocks * BLK)[:, None] + map_rows
        columns = jnp.where(map_rows < BLK, columns, VS).astype(jnp.int32)
        values = jnp.take(teacher_probs, row_ids.reshape(-1), axis=0).astype(jnp.float32)
        return mapped.at[columns.reshape(-1)].add(values, mode="drop")

    mapped = lax.fori_loop(0, OWNERS, add_owner, jnp.zeros((VS, TOK), jnp.float32))
    mass_totals = jnp.sum(mapped, axis=0)
    target = (mapped + smoothing / VS) / (mass_totals[None, :] + smoothing)
    logits_rows = lax.optimization_barrier(jnp.dot(hidden, student_weight, preferred_element_type=jnp.float32))
    student_logits = logits_rows.T
    student_lse = log_normalizer(student_logits)
    student_probs = jnp.exp(student_logits - student_lse[None, :])
    residual = (loss_scale * (student_probs - target)).astype(jnp.bfloat16)
    return jnp.dot(student_weight, residual, preferred_element_type=jnp.float32).astype(jnp.bfloat16)
```

```python
import functools

import jax
import jax.numpy as jnp
from jax import lax
from jax.experimental import pallas as pl
from jax.experimental.pallas import tpu as pltpu
from jax.sharding import PartitionSpec as P

BLK = 128
CAP = 2
META = 16
GROUP = 32
W_CHUNKS = 8

smoothing = 0.05
loss_scale = 64.0


def grid_of(owners):
    chips = owners // 2
    b = 1
    while (2 * b) * (2 * b) <= chips:
        b *= 2
    return chips // b, b


def kernel(
    n, A, B,
    tile_s, dest_s, block_s, hidden_hbm, w_hbm, codes_ref, exps_ref, map_ref, out_ref,
    w_ref, h_ref, tl_ref, probs_ref, send_ref, recv_ref, stat_send, tstat, sstat, mass, logits_ref, mapped_ref,
    res_ref, p_send, p_own, rc, rb, ra,
    w_sem, h_sem, a2a_send_sem, a2a_recv_sem, small_send_sem, small_recv_sem,
    c_send_sem, c_recv_sem, b_send_sem, b_recv_sem, a_send_sem, a_recv_sem,
):
    me = lax.axis_index("vocab")
    pairs = dest_s.shape[0]
    v_local = w_ref.shape[1]
    d_full = w_ref.shape[0]
    rows = d_full // n
    tokens = h_ref.shape[0]
    tiles = tl_ref.shape[0]
    payload = CAP * BLK
    core = lax.rem(me, 2)
    chip = me // 2
    b_me = lax.rem(chip, B)
    a_me = chip // B

    def at(a, b, c):
        return (a * B + b) * 2 + c

    barrier = pltpu.get_barrier_semaphore()

    def greet(off, carry):
        pl.semaphore_signal(barrier, inc=1, device_id={"vocab": lax.rem(me + off, n)}, device_id_type=pl.DeviceIdType.MESH)
        return carry

    lax.fori_loop(1, n, greet, 0)

    h_copy = pltpu.make_async_copy(hidden_hbm, h_ref, h_sem)
    h_copy.start()
    w_rows = d_full // W_CHUNKS
    w_copies = []
    for c in range(W_CHUNKS):
        part = pl.ds(c * w_rows, w_rows)
        w_copies.append(pltpu.make_async_copy(w_hbm.at[part, :], w_ref.at[part, :], w_sem.at[c]))
        w_copies[-1].start()

    exps = exps_ref[...]
    scales = jnp.where(exps >= 1, 2.0, jnp.where(exps == 0, 1.0, jnp.where(exps == -1, 0.5, 0.25)))
    per_tile = BLK // GROUP
    peak = jnp.full((1, tokens), -jnp.inf, jnp.float32)
    for t in range(tiles):
        codes = codes_ref[t * BLK:(t + 1) * BLK, :].astype(jnp.float32)
        scale = scales[t * per_tile:(t + 1) * per_tile, :]
        values = (codes.reshape(per_tile, GROUP, tokens) * scale[:, None, :]).reshape(BLK, tokens)
        tl_ref[t] = values.astype(jnp.bfloat16)
        peak = jnp.maximum(peak, jnp.max(values, axis=0, keepdims=True))
    total = jnp.zeros((1, tokens), jnp.float32)
    for t in range(tiles):
        total += jnp.sum(jnp.exp(tl_ref[t].astype(jnp.float32) - peak), axis=0, keepdims=True)

    row8 = lax.broadcasted_iota(jnp.int32, (8, tokens), 0)

    def small_copy(which, gathered, off):
        return pltpu.make_async_remote_copy(
            src_ref=stat_send.at[which],
            dst_ref=gathered.at[off],
            send_sem=small_send_sem.at[which],
            recv_sem=small_recv_sem.at[which],
            device_id={"vocab": lax.rem(me + off, n)},
            device_id_type=pl.DeviceIdType.MESH,
        )

    def share(which, gathered, tile):
        stat_send[which] = tile
        gathered[0] = tile

        def one(off, carry):
            small_copy(which, gathered, off).start()
            return carry

        lax.fori_loop(1, n, one, 0)

    def collect(which, gathered):
        others = gathered.at[pl.ds(1, n - 1)]
        pltpu.make_async_copy(others, others, small_recv_sem.at[which]).wait()

    def normalizer(gathered):
        peaks = gathered[:, 0, :]
        totals = gathered[:, 1, :]
        top = jnp.max(peaks, axis=0, keepdims=True)
        return top + jnp.log(jnp.sum(totals * jnp.exp(peaks - top), axis=0, keepdims=True))

    pl.semaphore_wait(barrier, n - 1)
    share(0, tstat, jnp.where(row8 == 0, peak, total))

    meta_row = lax.broadcasted_iota(jnp.int32, (META, BLK), 0)

    def fill(off, ref):
        target = lax.rem(me + off, n)

        def look(k, found):
            first, second = found
            hit = dest_s[k] == target
            second = jnp.where(hit & (first >= 0), k, second)
            first = jnp.where(hit & (first < 0), k, first)
            return first, second

        first, second = lax.fori_loop(0, pairs, look, (jnp.int32(-1), jnp.int32(-1)), unroll=8)
        meta = jnp.zeros((META, BLK), jnp.float32)
        for slot, source in enumerate((first, second)):
            index = jnp.maximum(source, 0)
            ref[off, slot * BLK:(slot + 1) * BLK, :] = tl_ref[tile_s[index]]
            entries = jnp.minimum(map_ref[pl.ds(index, 1), :], BLK)
            entries = jnp.where(source >= 0, entries, BLK).astype(jnp.float32)
            block = block_s[index].astype(jnp.float32)
            meta = jnp.where(meta_row == slot, entries, meta)
            meta = jnp.where(meta_row == CAP + slot, block, meta)
        ref[off, payload:payload + META, :] = meta.astype(jnp.bfloat16)

    def slot_copy(off):
        return pltpu.make_async_remote_copy(
            src_ref=send_ref.at[off],
            dst_ref=recv_ref.at[off],
            send_sem=a2a_send_sem,
            recv_sem=a2a_recv_sem.at[off],
            device_id={"vocab": lax.rem(me + off, n)},
            device_id_type=pl.DeviceIdType.MESH,
        )

    def send_slot(off, carry):
        fill(off, send_ref)
        slot_copy(off).start()
        return carry

    lax.fori_loop(1, n, send_slot, 0)
    fill(0, recv_ref)

    h_copy.wait()
    logits = jnp.zeros((tokens, v_local), jnp.float32)
    for c in range(W_CHUNKS):
        w_copies[c].wait()
        logits += jnp.dot(
            h_ref[:, c * w_rows:(c + 1) * w_rows],
            w_ref[c * w_rows:(c + 1) * w_rows, :],
            preferred_element_type=jnp.float32,
        )
    logits = logits.T
    logits_ref[...] = logits
    s_peak = jnp.max(logits, axis=0, keepdims=True)
    s_total = jnp.sum(jnp.exp(logits - s_peak), axis=0, keepdims=True)
    share(1, sstat, jnp.where(row8 == 0, s_peak, s_total))

    collect(0, tstat)
    lse = normalizer(tstat)
    tile_row = lax.broadcasted_iota(jnp.int32, (tiles, BLK), 0)

    def count(k, counts):
        valid = jnp.where(map_ref[pl.ds(k, 1), :] < BLK, 1.0, 0.0)
        return counts + jnp.where(tile_row == tile_s[k], valid, 0.0)

    counts = lax.fori_loop(0, pairs, count, jnp.zeros((tiles, BLK), jnp.float32))
    counts = counts.astype(jnp.bfloat16)
    part_mass = jnp.zeros((tiles, tokens), jnp.float32)
    for t in range(tiles):
        probs = jnp.exp(tl_ref[t].astype(jnp.float32) - lse).astype(jnp.bfloat16)
        term = jnp.dot(counts, probs, preferred_element_type=jnp.float32)
        part_mass += jnp.where(lax.broadcasted_iota(jnp.int32, (tiles, tokens), 0) == t, term, 0.0)
    part_mass = jnp.sum(part_mass, axis=0, keepdims=True)
    share(2, mass, jnp.broadcast_to(part_mass, (8, tokens)))

    mapped_ref[...] = jnp.zeros_like(mapped_ref)
    entry = lax.broadcasted_iota(jnp.int32, (v_local, BLK), 0).astype(jnp.float32)

    def join(off):
        probs_ref[...] = jnp.exp(recv_ref[off, 0:payload, :].astype(jnp.float32) - lse).astype(jnp.bfloat16)
        meta = recv_ref[off, payload:payload + META, :].astype(jnp.float32)
        pickers = []
        for slot in range(CAP):
            entries = meta[slot:slot + 1, :]
            blocks = meta[CAP + slot:CAP + slot + 1, :]
            places = jnp.where(entries < BLK, blocks * BLK + entries, float(v_local))
            pickers.append(jnp.where(entry == places, 1.0, 0.0).astype(jnp.bfloat16))
        picker = jnp.concatenate(pickers, axis=1)
        mapped_ref[...] += jnp.dot(picker, probs_ref[...], preferred_element_type=jnp.float32)

    join(0)

    def join_next(off, carry):
        slot_copy(off).wait_recv()
        join(off)
        return carry

    lax.fori_loop(1, n, join_next, 0)

    collect(1, sstat)
    collect(2, mass)
    s_lse = normalizer(sstat)
    mass_total = jnp.sum(mass[:, 0, :], axis=0, keepdims=True)
    target = (mapped_ref[...] + smoothing / (v_local * n)) / (mass_total + smoothing)
    s_probs = jnp.exp(logits_ref[...] - s_lse)
    res_ref[...] = (loss_scale * (s_probs - target)).astype(jnp.bfloat16)

    def core_copy(i, j):
        idx = i * B + j
        return pltpu.make_async_remote_copy(
            src_ref=p_send.at[idx], dst_ref=rc.at[idx],
            send_sem=c_send_sem, recv_sem=c_recv_sem.at[idx],
            device_id={"vocab": at(a_me, b_me, 1 - core)}, device_id_type=pl.DeviceIdType.MESH,
        )

    def b_copy(i, j):
        return pltpu.make_async_remote_copy(
            src_ref=p_own.at[i * B + j], dst_ref=rb.at[i * (B - 1) + j],
            send_sem=b_send_sem, recv_sem=b_recv_sem.at[i * (B - 1) + j],
            device_id={"vocab": at(a_me, lax.rem(b_me + 1 + j, B), core)}, device_id_type=pl.DeviceIdType.MESH,
        )

    def a_copy(i):
        return pltpu.make_async_remote_copy(
            src_ref=p_own.at[i * B + B - 1], dst_ref=ra.at[i],
            send_sem=a_send_sem, recv_sem=a_recv_sem.at[i],
            device_id={"vocab": at(lax.rem(a_me + 1 + i, A), b_me, core)}, device_id_type=pl.DeviceIdType.MESH,
        )

    def product(i, j, c):
        owner = at(lax.rem(a_me + 1 + i, A), lax.rem(b_me + 1 + j, B), c)
        start = pl.multiple_of(owner * rows, rows)
        return jnp.dot(w_ref[pl.ds(start, rows), :], res_ref[...], preferred_element_type=jnp.float32)

    for i in range(A + 2):
        if i < A:
            def produce(j, carry, i=i):
                p_send[i * B + j] = product(i, j, 1 - core)
                core_copy(i, j).start()
                p_own[i * B + j] = product(i, j, core)
                return carry

            lax.fori_loop(0, B, produce, 0)
        if 1 <= i <= A:
            q = i - 1
            for j in range(B):
                core_copy(q, j).wait_recv()
                p_own[q * B + j] += rc[q * B + j]
                if j < B - 1:
                    b_copy(q, j).start()
        if i >= 2:
            q = i - 2
            acc = p_own[q * B + B - 1]
            for j in range(B - 1):
                b_copy(q, j).wait_recv()
                acc += rb[q * (B - 1) + j]
            p_own[q * B + B - 1] = acc
            if q < A - 1:
                a_copy(q).start()

    acc = p_own[A * B - 1]
    for i in range(A - 1):
        a_copy(i).wait_recv()
        acc += ra[i]
    out_ref[...] = acc.astype(jnp.bfloat16)

    def drained(ref, sem):
        pltpu.make_async_copy(ref, ref, sem).wait()

    drained(send_ref.at[pl.ds(1, n - 1)], a2a_send_sem)
    for which, gathered in enumerate((tstat, sstat, mass)):
        drained(gathered.at[pl.ds(1, n - 1)], small_send_sem.at[which])
    drained(p_send, c_send_sem)
    drained(rb, b_send_sem)
    drained(ra, a_send_sem)


def per_device(
    n, hidden, student_weight, teacher_codes, teacher_exps, pair_tile, pair_dest, pair_block, pair_map
):
    A, B = grid_of(n)
    tokens, d_full = hidden.shape
    v_local = student_weight.shape[1]
    rows = d_full // n
    tiles = teacher_codes.shape[0] // BLK
    slot_rows = CAP * BLK + META
    f32, bf16 = jnp.float32, jnp.bfloat16
    vmem = pl.BlockSpec(memory_space=pltpu.VMEM)
    smem = pl.BlockSpec(memory_space=pltpu.SMEM)
    hbm = pl.BlockSpec(memory_space=pl.ANY)
    dma = pltpu.SemaphoreType.DMA
    return pl.pallas_call(
        functools.partial(kernel, n, A, B),
        out_shape=jax.ShapeDtypeStruct((rows, tokens), bf16),
        in_specs=[smem, smem, smem, hbm, hbm, vmem, vmem, vmem],
        out_specs=vmem,
        scratch_shapes=[
            pltpu.VMEM((d_full, v_local), bf16),
            pltpu.VMEM((tokens, d_full), bf16),
            pltpu.VMEM((tiles, BLK, tokens), bf16),
            pltpu.VMEM((CAP * BLK, tokens), bf16),
            pltpu.VMEM((n, slot_rows, tokens), bf16),
            pltpu.VMEM((n, slot_rows, tokens), bf16),
            pltpu.VMEM((3, 8, tokens), f32),
            pltpu.VMEM((n, 8, tokens), f32),
            pltpu.VMEM((n, 8, tokens), f32),
            pltpu.VMEM((n, 8, tokens), f32),
            pltpu.VMEM((v_local, tokens), f32),
            pltpu.VMEM((v_local, tokens), f32),
            pltpu.VMEM((v_local, tokens), bf16),
            pltpu.VMEM((A * B, rows, tokens), f32),
            pltpu.VMEM((A * B, rows, tokens), f32),
            pltpu.VMEM((A * B, rows, tokens), f32),
            pltpu.VMEM((A * (B - 1), rows, tokens), f32),
            pltpu.VMEM((A - 1, rows, tokens), f32),
            dma((W_CHUNKS,)),
            dma,
            dma,
            dma((n,)),
            dma((3,)),
            dma((3,)),
            dma,
            dma((A * B,)),
            dma,
            dma((A * (B - 1),)),
            dma,
            dma((A - 1,)),
        ],
        compiler_params=pltpu.CompilerParams(
            collective_id=0, has_side_effects=True, vmem_limit_bytes=56 * 1024 * 1024
        ),
    )(
        pair_tile, pair_dest.reshape(-1), pair_block,
        hidden, student_weight, teacher_codes, teacher_exps, pair_map,
    )


def solution(mesh):
    return jax.shard_map(
        functools.partial(per_device, mesh.shape["vocab"]),
        mesh=mesh,
        in_specs=(
            P("groups", None),
            P(None, "vocab"),
            P("vocab", "groups"),
            P("vocab", "groups"),
            P("vocab"),
            P("vocab", None),
            P("vocab"),
            P("vocab", None),
        ),
        out_specs=P("vocab", "groups"),
        check_vma=False,
    )
```

```python
import functools

import jax
import jax.numpy as jnp
from jax import lax
from jax.experimental import pallas as pl
from jax.experimental.pallas import tpu as pltpu
from jax.sharding import PartitionSpec as P

BLK = 128
CAP = 2
META = 16
GROUP = 32
W_CHUNKS = 8
SCALE_ROWS = 16
TOP_CODE = 32000.0
TINY = 1e-30

smoothing = 0.05
loss_scale = 64.0


def grid_of(owners):
    chips = owners // 2
    b = 1
    while (2 * b) * (2 * b) <= chips:
        b *= 2
    return chips // b, b


def encode(values, ref):
    rows = values.shape[0]
    top = jnp.maximum(jnp.max(jnp.abs(values), axis=0, keepdims=True), TINY)
    level = jnp.ceil(8.0 * jnp.log2(top))
    step = TOP_CODE / jnp.exp2(level * 0.125)
    codes = jnp.round(values * step).astype(jnp.int32)
    ref[0:rows, :] = codes.astype(jnp.int16)
    levels = jnp.broadcast_to(level, (SCALE_ROWS, values.shape[1])).astype(jnp.int32)
    ref[rows:rows + SCALE_ROWS, :] = levels.astype(jnp.int16)


def decode(ref):
    rows = ref.shape[0] - SCALE_ROWS
    level = ref[rows:rows + SCALE_ROWS, :].astype(jnp.int32).astype(jnp.float32)[0:1, :]
    scale = jnp.exp2(level * 0.125) * (1.0 / TOP_CODE)
    return ref[0:rows, :].astype(jnp.int32).astype(jnp.float32) * scale


def kernel(
    n, A, B,
    tile_s, dest_s, block_s, hidden_hbm, w_hbm, codes_ref, exps_ref, map_ref, out_ref,
    w_ref, h_ref, tl_ref, probs_ref, send_ref, recv_ref, stat_send, tstat, sstat, mass, logits_ref, mapped_ref,
    res_ref, p_send, p_own, rc, sb, sa, rb, ra,
    w_sem, h_sem, a2a_send_sem, a2a_recv_sem, small_send_sem, small_recv_sem,
    c_send_sem, c_recv_sem, b_send_sem, b_recv_sem, a_send_sem, a_recv_sem,
):
    me = lax.axis_index("vocab")
    pairs = dest_s.shape[0]
    v_local = w_ref.shape[1]
    d_full = w_ref.shape[0]
    rows = d_full // n
    tokens = h_ref.shape[0]
    tiles = tl_ref.shape[0]
    payload = CAP * BLK
    core = lax.rem(me, 2)
    chip = me // 2
    b_me = lax.rem(chip, B)
    a_me = chip // B

    def at(a, b, c):
        return (a * B + b) * 2 + c

    barrier = pltpu.get_barrier_semaphore()

    def greet(off, carry):
        pl.semaphore_signal(barrier, inc=1, device_id={"vocab": lax.rem(me + off, n)}, device_id_type=pl.DeviceIdType.MESH)
        return carry

    lax.fori_loop(1, n, greet, 0)

    h_copy = pltpu.make_async_copy(hidden_hbm, h_ref, h_sem)
    h_copy.start()
    w_rows = d_full // W_CHUNKS
    w_copies = []
    for c in range(W_CHUNKS):
        part = pl.ds(c * w_rows, w_rows)
        w_copies.append(pltpu.make_async_copy(w_hbm.at[part, :], w_ref.at[part, :], w_sem.at[c]))
        w_copies[-1].start()

    exps = exps_ref[...]
    scales = jnp.where(exps >= 1, 2.0, jnp.where(exps == 0, 1.0, jnp.where(exps == -1, 0.5, 0.25)))
    per_tile = BLK // GROUP
    peak = jnp.full((1, tokens), -jnp.inf, jnp.float32)
    for t in range(tiles):
        codes = codes_ref[t * BLK:(t + 1) * BLK, :].astype(jnp.float32)
        scale = scales[t * per_tile:(t + 1) * per_tile, :]
        values = (codes.reshape(per_tile, GROUP, tokens) * scale[:, None, :]).reshape(BLK, tokens)
        tl_ref[t] = values.astype(jnp.bfloat16)
        peak = jnp.maximum(peak, jnp.max(values, axis=0, keepdims=True))
    total = jnp.zeros((1, tokens), jnp.float32)
    for t in range(tiles):
        total += jnp.sum(jnp.exp(tl_ref[t].astype(jnp.float32) - peak), axis=0, keepdims=True)

    row8 = lax.broadcasted_iota(jnp.int32, (8, tokens), 0)

    def small_copy(which, gathered, off):
        return pltpu.make_async_remote_copy(
            src_ref=stat_send.at[which],
            dst_ref=gathered.at[off],
            send_sem=small_send_sem.at[which],
            recv_sem=small_recv_sem.at[which],
            device_id={"vocab": lax.rem(me + off, n)},
            device_id_type=pl.DeviceIdType.MESH,
        )

    def share(which, gathered, tile):
        stat_send[which] = tile
        gathered[0] = tile

        def one(off, carry):
            small_copy(which, gathered, off).start()
            return carry

        lax.fori_loop(1, n, one, 0)

    def collect(which, gathered):
        others = gathered.at[pl.ds(1, n - 1)]
        pltpu.make_async_copy(others, others, small_recv_sem.at[which]).wait()

    def normalizer(gathered):
        peaks = gathered[:, 0, :]
        totals = gathered[:, 1, :]
        top = jnp.max(peaks, axis=0, keepdims=True)
        return top + jnp.log(jnp.sum(totals * jnp.exp(peaks - top), axis=0, keepdims=True))

    pl.semaphore_wait(barrier, n - 1)
    share(0, tstat, jnp.where(row8 == 0, peak, total))

    meta_row = lax.broadcasted_iota(jnp.int32, (META, BLK), 0)

    def fill(off, ref):
        target = lax.rem(me + off, n)

        def look(k, found):
            first, second = found
            hit = dest_s[k] == target
            second = jnp.where(hit & (first >= 0), k, second)
            first = jnp.where(hit & (first < 0), k, first)
            return first, second

        first, second = lax.fori_loop(0, pairs, look, (jnp.int32(-1), jnp.int32(-1)), unroll=8)
        meta = jnp.zeros((META, BLK), jnp.float32)
        for slot, source in enumerate((first, second)):
            index = jnp.maximum(source, 0)
            ref[off, slot * BLK:(slot + 1) * BLK, :] = tl_ref[tile_s[index]]
            entries = jnp.minimum(map_ref[pl.ds(index, 1), :], BLK)
            entries = jnp.where(source >= 0, entries, BLK).astype(jnp.float32)
            block = block_s[index].astype(jnp.float32)
            meta = jnp.where(meta_row == slot, entries, meta)
            meta = jnp.where(meta_row == CAP + slot, block, meta)
        ref[off, payload:payload + META, :] = meta.astype(jnp.bfloat16)

    def slot_copy(off):
        return pltpu.make_async_remote_copy(
            src_ref=send_ref.at[off],
            dst_ref=recv_ref.at[off],
            send_sem=a2a_send_sem,
            recv_sem=a2a_recv_sem.at[off],
            device_id={"vocab": lax.rem(me + off, n)},
            device_id_type=pl.DeviceIdType.MESH,
        )

    def far_first(i):
        odd = lax.rem(i, 2)
        return n // 2 + odd * ((i + 1) // 2) - (1 - odd) * (i // 2)

    def send_slot(i, carry):
        off = far_first(i)
        fill(off, send_ref)
        slot_copy(off).start()
        return carry

    lax.fori_loop(0, n - 1, send_slot, 0)
    fill(0, recv_ref)

    h_copy.wait()
    logits = jnp.zeros((tokens, v_local), jnp.float32)
    for c in range(W_CHUNKS):
        w_copies[c].wait()
        logits += jnp.dot(
            h_ref[:, c * w_rows:(c + 1) * w_rows],
            w_ref[c * w_rows:(c + 1) * w_rows, :],
            preferred_element_type=jnp.float32,
        )
    logits = logits.T
    logits_ref[...] = logits
    s_peak = jnp.max(logits, axis=0, keepdims=True)
    s_total = jnp.sum(jnp.exp(logits - s_peak), axis=0, keepdims=True)
    share(1, sstat, jnp.where(row8 == 0, s_peak, s_total))

    collect(0, tstat)
    lse = normalizer(tstat)
    tile_row = lax.broadcasted_iota(jnp.int32, (tiles, BLK), 0)

    def count(k, counts):
        valid = jnp.where(map_ref[pl.ds(k, 1), :] < BLK, 1.0, 0.0)
        return counts + jnp.where(tile_row == tile_s[k], valid, 0.0)

    counts = lax.fori_loop(0, pairs, count, jnp.zeros((tiles, BLK), jnp.float32))
    counts = counts.astype(jnp.bfloat16)
    part_mass = jnp.zeros((tiles, tokens), jnp.float32)
    for t in range(tiles):
        probs = jnp.exp(tl_ref[t].astype(jnp.float32) - lse).astype(jnp.bfloat16)
        term = jnp.dot(counts, probs, preferred_element_type=jnp.float32)
        part_mass += jnp.where(lax.broadcasted_iota(jnp.int32, (tiles, tokens), 0) == t, term, 0.0)
    part_mass = jnp.sum(part_mass, axis=0, keepdims=True)
    share(2, mass, jnp.broadcast_to(part_mass, (8, tokens)))

    mapped_ref[...] = jnp.zeros_like(mapped_ref)
    entry = lax.broadcasted_iota(jnp.int32, (v_local, BLK), 0).astype(jnp.float32)

    def join(off):
        probs_ref[...] = jnp.exp(recv_ref[off, 0:payload, :].astype(jnp.float32) - lse).astype(jnp.bfloat16)
        meta = recv_ref[off, payload:payload + META, :].astype(jnp.float32)
        pickers = []
        for slot in range(CAP):
            entries = meta[slot:slot + 1, :]
            blocks = meta[CAP + slot:CAP + slot + 1, :]
            places = jnp.where(entries < BLK, blocks * BLK + entries, float(v_local))
            pickers.append(jnp.where(entry == places, 1.0, 0.0).astype(jnp.bfloat16))
        picker = jnp.concatenate(pickers, axis=1)
        mapped_ref[...] += jnp.dot(picker, probs_ref[...], preferred_element_type=jnp.float32)

    join(0)

    def join_next(i, carry):
        off = far_first(i)
        slot_copy(off).wait_recv()
        join(off)
        return carry

    lax.fori_loop(0, n - 1, join_next, 0)

    collect(1, sstat)
    collect(2, mass)
    s_lse = normalizer(sstat)
    mass_total = jnp.sum(mass[:, 0, :], axis=0, keepdims=True)
    target = (mapped_ref[...] + smoothing / (v_local * n)) / (mass_total + smoothing)
    s_probs = jnp.exp(logits_ref[...] - s_lse)
    res_ref[...] = (loss_scale * (s_probs - target)).astype(jnp.bfloat16)

    def core_copy(i, j):
        idx = i * B + j
        return pltpu.make_async_remote_copy(
            src_ref=p_send.at[idx], dst_ref=rc.at[idx],
            send_sem=c_send_sem, recv_sem=c_recv_sem.at[idx],
            device_id={"vocab": at(a_me, b_me, 1 - core)}, device_id_type=pl.DeviceIdType.MESH,
        )

    def b_copy(i, j):
        return pltpu.make_async_remote_copy(
            src_ref=sb.at[i * (B - 1) + j], dst_ref=rb.at[i * (B - 1) + j],
            send_sem=b_send_sem, recv_sem=b_recv_sem.at[i * (B - 1) + j],
            device_id={"vocab": at(a_me, lax.rem(b_me + 1 + j, B), core)}, device_id_type=pl.DeviceIdType.MESH,
        )

    def a_copy(i):
        return pltpu.make_async_remote_copy(
            src_ref=sa.at[i], dst_ref=ra.at[i],
            send_sem=a_send_sem, recv_sem=a_recv_sem.at[i],
            device_id={"vocab": at(lax.rem(a_me + 1 + i, A), b_me, core)}, device_id_type=pl.DeviceIdType.MESH,
        )

    def product(i, j, c):
        owner = at(lax.rem(a_me + 1 + i, A), lax.rem(b_me + 1 + j, B), c)
        start = pl.multiple_of(owner * rows, rows)
        return jnp.dot(w_ref[pl.ds(start, rows), :], res_ref[...], preferred_element_type=jnp.float32)

    for i in range(A + 2):
        if i < A:
            def produce(j, carry, i=i):
                p_send[i * B + j] = product(i, j, 1 - core)
                core_copy(i, j).start()
                p_own[i * B + j] = product(i, j, core)
                return carry

            lax.fori_loop(0, B, produce, 0)
        if 1 <= i <= A:
            q = i - 1
            for j in range(B):
                core_copy(q, j).wait_recv()
                both = p_own[q * B + j] + rc[q * B + j]
                if j < B - 1:
                    encode(both, sb.at[q * (B - 1) + j])
                    b_copy(q, j).start()
                else:
                    p_own[q * B + j] = both
        if i >= 2:
            q = i - 2
            acc = p_own[q * B + B - 1]
            for j in range(B - 1):
                b_copy(q, j).wait_recv()
                acc += decode(rb.at[q * (B - 1) + j])
            if q < A - 1:
                encode(acc, sa.at[q])
                a_copy(q).start()

    for i in range(A - 1):
        a_copy(i).wait_recv()
        acc += decode(ra.at[i])
    out_ref[...] = acc.astype(jnp.bfloat16)

    def drained(ref, sem):
        pltpu.make_async_copy(ref, ref, sem).wait()

    drained(send_ref.at[pl.ds(1, n - 1)], a2a_send_sem)
    for which, gathered in enumerate((tstat, sstat, mass)):
        drained(gathered.at[pl.ds(1, n - 1)], small_send_sem.at[which])
    drained(p_send, c_send_sem)
    drained(rb, b_send_sem)
    drained(ra, a_send_sem)


def per_device(
    n, hidden, student_weight, teacher_codes, teacher_exps, pair_tile, pair_dest, pair_block, pair_map
):
    A, B = grid_of(n)
    tokens, d_full = hidden.shape
    v_local = student_weight.shape[1]
    rows = d_full // n
    tiles = teacher_codes.shape[0] // BLK
    slot_rows = CAP * BLK + META
    f32, bf16 = jnp.float32, jnp.bfloat16
    vmem = pl.BlockSpec(memory_space=pltpu.VMEM)
    smem = pl.BlockSpec(memory_space=pltpu.SMEM)
    hbm = pl.BlockSpec(memory_space=pl.ANY)
    dma = pltpu.SemaphoreType.DMA
    return pl.pallas_call(
        functools.partial(kernel, n, A, B),
        out_shape=jax.ShapeDtypeStruct((rows, tokens), bf16),
        in_specs=[smem, smem, smem, hbm, hbm, vmem, vmem, vmem],
        out_specs=vmem,
        scratch_shapes=[
            pltpu.VMEM((d_full, v_local), bf16),
            pltpu.VMEM((tokens, d_full), bf16),
            pltpu.VMEM((tiles, BLK, tokens), bf16),
            pltpu.VMEM((CAP * BLK, tokens), bf16),
            pltpu.VMEM((n, slot_rows, tokens), bf16),
            pltpu.VMEM((n, slot_rows, tokens), bf16),
            pltpu.VMEM((3, 8, tokens), f32),
            pltpu.VMEM((n, 8, tokens), f32),
            pltpu.VMEM((n, 8, tokens), f32),
            pltpu.VMEM((n, 8, tokens), f32),
            pltpu.VMEM((v_local, tokens), f32),
            pltpu.VMEM((v_local, tokens), f32),
            pltpu.VMEM((v_local, tokens), bf16),
            pltpu.VMEM((A * B, rows, tokens), f32),
            pltpu.VMEM((A * B, rows, tokens), f32),
            pltpu.VMEM((A * B, rows, tokens), f32),
            pltpu.VMEM((A * (B - 1), rows + SCALE_ROWS, tokens), jnp.int16),
            pltpu.VMEM((A - 1, rows + SCALE_ROWS, tokens), jnp.int16),
            pltpu.VMEM((A * (B - 1), rows + SCALE_ROWS, tokens), jnp.int16),
            pltpu.VMEM((A - 1, rows + SCALE_ROWS, tokens), jnp.int16),
            dma((W_CHUNKS,)),
            dma,
            dma,
            dma((n,)),
            dma((3,)),
            dma((3,)),
            dma,
            dma((A * B,)),
            dma,
            dma((A * (B - 1),)),
            dma,
            dma((A - 1,)),
        ],
        compiler_params=pltpu.CompilerParams(
            collective_id=0, has_side_effects=True, vmem_limit_bytes=56 * 1024 * 1024
        ),
    )(
        pair_tile, pair_dest.reshape(-1), pair_block,
        hidden, student_weight, teacher_codes, teacher_exps, pair_map,
    )


def solution(mesh):
    return jax.shard_map(
        functools.partial(per_device, mesh.shape["vocab"]),
        mesh=mesh,
        in_specs=(
            P("groups", None),
            P(None, "vocab"),
            P("vocab", "groups"),
            P("vocab", "groups"),
            P("vocab"),
            P("vocab", None),
            P("vocab"),
            P("vocab", None),
        ),
        out_specs=P("vocab", "groups"),
        check_vma=False,
    )
```

```python
import functools

import jax
import jax.numpy as jnp
from jax import lax
from jax.experimental import pallas as pl
from jax.experimental.pallas import tpu as pltpu
from jax.sharding import PartitionSpec as P

BLK = 128
CAP = 2
META = 16
GROUP = 32
W_CHUNKS = 8
SCALE_ROWS = 16
CUTS = 1
TOP_CODE = 32000.0
TINY = 1e-30

smoothing = 0.05
loss_scale = 64.0


def grid_of(owners):
    chips = owners // 2
    b = 1
    while (2 * b) * (2 * b) <= chips:
        b *= 2
    return chips // b, b


def encode(values, ref):
    rows = values.shape[0]
    top = jnp.maximum(jnp.max(jnp.abs(values), axis=0, keepdims=True), TINY)
    level = jnp.ceil(8.0 * jnp.log2(top))
    step = TOP_CODE / jnp.exp2(level * 0.125)
    codes = jnp.round(values * step).astype(jnp.int32)
    ref[0:rows, :] = codes.astype(jnp.int16)
    levels = jnp.broadcast_to(level, (SCALE_ROWS, values.shape[1])).astype(jnp.int32)
    ref[rows:rows + SCALE_ROWS, :] = levels.astype(jnp.int16)


def decode(ref):
    rows = ref.shape[0] - SCALE_ROWS
    level = ref[rows:rows + SCALE_ROWS, :].astype(jnp.int32).astype(jnp.float32)[0:1, :]
    scale = jnp.exp2(level * 0.125) * (1.0 / TOP_CODE)
    return ref[0:rows, :].astype(jnp.int32).astype(jnp.float32) * scale


def kernel(
    n, A, B,
    tile_s, dest_s, block_s, hidden_hbm, w_hbm, codes_ref, exps_ref, map_ref, out_ref,
    w_ref, h_ref, tl_ref, probs_ref, send_ref, recv_ref, stat_send, tstat, sstat, mass, logits_ref, mapped_ref,
    res_ref, p_send, p_own, rc, sb, sa, rb, ra,
    w_sem, h_sem, a2a_send_sem, a2a_recv_sem, small_send_sem, small_recv_sem,
    c_send_sem, c_recv_sem, b_send_sem, b_recv_sem, a_send_sem, a_recv_sem,
):
    me = lax.axis_index("vocab")
    pairs = dest_s.shape[0]
    v_local = w_ref.shape[1]
    d_full = w_ref.shape[0]
    rows = d_full // n
    tokens = h_ref.shape[0]
    tiles = tl_ref.shape[0]
    payload = CAP * BLK
    core = lax.rem(me, 2)
    chip = me // 2
    b_me = lax.rem(chip, B)
    a_me = chip // B

    def at(a, b, c):
        return (a * B + b) * 2 + c

    barrier = pltpu.get_barrier_semaphore()

    def greet(off, carry):
        pl.semaphore_signal(barrier, inc=1, device_id={"vocab": lax.rem(me + off, n)}, device_id_type=pl.DeviceIdType.MESH)
        return carry

    lax.fori_loop(1, n, greet, 0)

    h_copy = pltpu.make_async_copy(hidden_hbm, h_ref, h_sem)
    h_copy.start()
    w_rows = d_full // W_CHUNKS
    w_copies = []
    for c in range(W_CHUNKS):
        part = pl.ds(c * w_rows, w_rows)
        w_copies.append(pltpu.make_async_copy(w_hbm.at[part, :], w_ref.at[part, :], w_sem.at[c]))
        w_copies[-1].start()

    exps = exps_ref[...]
    scales = jnp.where(exps >= 1, 2.0, jnp.where(exps == 0, 1.0, jnp.where(exps == -1, 0.5, 0.25)))
    per_tile = BLK // GROUP
    peak = jnp.full((1, tokens), -jnp.inf, jnp.float32)
    for t in range(tiles):
        codes = codes_ref[t * BLK:(t + 1) * BLK, :].astype(jnp.float32)
        scale = scales[t * per_tile:(t + 1) * per_tile, :]
        values = (codes.reshape(per_tile, GROUP, tokens) * scale[:, None, :]).reshape(BLK, tokens)
        tl_ref[t] = values.astype(jnp.bfloat16)
        peak = jnp.maximum(peak, jnp.max(values, axis=0, keepdims=True))
    total = jnp.zeros((1, tokens), jnp.float32)
    for t in range(tiles):
        total += jnp.sum(jnp.exp(tl_ref[t].astype(jnp.float32) - peak), axis=0, keepdims=True)

    row8 = lax.broadcasted_iota(jnp.int32, (8, tokens), 0)

    def small_copy(which, gathered, off):
        return pltpu.make_async_remote_copy(
            src_ref=stat_send.at[which],
            dst_ref=gathered.at[off],
            send_sem=small_send_sem.at[which],
            recv_sem=small_recv_sem.at[which],
            device_id={"vocab": lax.rem(me + off, n)},
            device_id_type=pl.DeviceIdType.MESH,
        )

    def share(which, gathered, tile):
        stat_send[which] = tile
        gathered[0] = tile

        def one(off, carry):
            small_copy(which, gathered, off).start()
            return carry

        lax.fori_loop(1, n, one, 0)

    def collect(which, gathered):
        others = gathered.at[pl.ds(1, n - 1)]
        pltpu.make_async_copy(others, others, small_recv_sem.at[which]).wait()

    def normalizer(gathered):
        peaks = gathered[:, 0, :]
        totals = gathered[:, 1, :]
        top = jnp.max(peaks, axis=0, keepdims=True)
        return top + jnp.log(jnp.sum(totals * jnp.exp(peaks - top), axis=0, keepdims=True))

    pl.semaphore_wait(barrier, n - 1)
    share(0, tstat, jnp.where(row8 == 0, peak, total))

    meta_row = lax.broadcasted_iota(jnp.int32, (META, BLK), 0)

    def fill(off, ref):
        target = lax.rem(me + off, n)

        def look(k, found):
            first, second = found
            hit = dest_s[k] == target
            second = jnp.where(hit & (first >= 0), k, second)
            first = jnp.where(hit & (first < 0), k, first)
            return first, second

        first, second = lax.fori_loop(0, pairs, look, (jnp.int32(-1), jnp.int32(-1)), unroll=8)
        meta = jnp.zeros((META, BLK), jnp.float32)
        for slot, source in enumerate((first, second)):
            index = jnp.maximum(source, 0)
            ref[off, slot * BLK:(slot + 1) * BLK, :] = tl_ref[tile_s[index]]
            entries = jnp.minimum(map_ref[pl.ds(index, 1), :], BLK)
            entries = jnp.where(source >= 0, entries, BLK).astype(jnp.float32)
            block = block_s[index].astype(jnp.float32)
            meta = jnp.where(meta_row == slot, entries, meta)
            meta = jnp.where(meta_row == CAP + slot, block, meta)
        ref[off, payload:payload + META, :] = meta.astype(jnp.bfloat16)

    def slot_copy(off):
        return pltpu.make_async_remote_copy(
            src_ref=send_ref.at[off],
            dst_ref=recv_ref.at[off],
            send_sem=a2a_send_sem,
            recv_sem=a2a_recv_sem.at[off],
            device_id={"vocab": lax.rem(me + off, n)},
            device_id_type=pl.DeviceIdType.MESH,
        )

    def spread(i, size):
        odd = lax.rem(i, 2)
        return size // 2 + odd * ((i + 1) // 2) - (1 - odd) * (i // 2)

    def slot_order(i):
        odd = lax.rem(i, 2)
        return spread(odd * (n - 2 - i // 2) + (1 - odd) * (i // 2), n)

    def send_slot(i, carry):
        off = slot_order(i)
        fill(off, send_ref)
        slot_copy(off).start()
        return carry

    early = n // 3
    lax.fori_loop(0, early, send_slot, 0)

    h_copy.wait()
    logits = jnp.zeros((tokens, v_local), jnp.float32)
    for c in range(W_CHUNKS):
        w_copies[c].wait()
        logits += jnp.dot(
            h_ref[:, c * w_rows:(c + 1) * w_rows],
            w_ref[c * w_rows:(c + 1) * w_rows, :],
            preferred_element_type=jnp.float32,
        )
    logits = logits.T
    logits_ref[...] = logits
    s_peak = jnp.max(logits, axis=0, keepdims=True)
    s_total = jnp.sum(jnp.exp(logits - s_peak), axis=0, keepdims=True)
    share(1, sstat, jnp.where(row8 == 0, s_peak, s_total))

    collect(0, tstat)
    lse = normalizer(tstat)
    tile_row = lax.broadcasted_iota(jnp.int32, (tiles, BLK), 0)

    def count(k, counts):
        valid = jnp.where(map_ref[pl.ds(k, 1), :] < BLK, 1.0, 0.0)
        return counts + jnp.where(tile_row == tile_s[k], valid, 0.0)

    counts = lax.fori_loop(0, pairs, count, jnp.zeros((tiles, BLK), jnp.float32))
    counts = counts.astype(jnp.bfloat16)
    part_mass = jnp.zeros((tiles, tokens), jnp.float32)
    for t in range(tiles):
        probs = jnp.exp(tl_ref[t].astype(jnp.float32) - lse).astype(jnp.bfloat16)
        term = jnp.dot(counts, probs, preferred_element_type=jnp.float32)
        part_mass += jnp.where(lax.broadcasted_iota(jnp.int32, (tiles, tokens), 0) == t, term, 0.0)
    part_mass = jnp.sum(part_mass, axis=0, keepdims=True)
    share(2, mass, jnp.broadcast_to(part_mass, (8, tokens)))

    lax.fori_loop(early, n - 1, send_slot, 0)
    fill(0, recv_ref)

    mapped_ref[...] = jnp.zeros_like(mapped_ref)
    entry = lax.broadcasted_iota(jnp.int32, (v_local, BLK), 0).astype(jnp.float32)

    def join(off):
        probs_ref[...] = jnp.exp(recv_ref[off, 0:payload, :].astype(jnp.float32) - lse).astype(jnp.bfloat16)
        meta = recv_ref[off, payload:payload + META, :].astype(jnp.float32)
        pickers = []
        for slot in range(CAP):
            entries = meta[slot:slot + 1, :]
            blocks = meta[CAP + slot:CAP + slot + 1, :]
            places = jnp.where(entries < BLK, blocks * BLK + entries, float(v_local))
            pickers.append(jnp.where(entry == places, 1.0, 0.0).astype(jnp.bfloat16))
        picker = jnp.concatenate(pickers, axis=1)
        mapped_ref[...] += jnp.dot(picker, probs_ref[...], preferred_element_type=jnp.float32)

    join(0)

    def join_next(i, carry):
        off = slot_order(i)
        slot_copy(off).wait_recv()
        join(off)
        return carry

    lax.fori_loop(0, n - 1, join_next, 0)

    collect(1, sstat)
    collect(2, mass)
    s_lse = normalizer(sstat)
    mass_total = jnp.sum(mass[:, 0, :], axis=0, keepdims=True)
    target = (mapped_ref[...] + smoothing / (v_local * n)) / (mass_total + smoothing)
    s_probs = jnp.exp(logits_ref[...] - s_lse)
    res_ref[...] = (loss_scale * (s_probs - target)).astype(jnp.bfloat16)

    cut = rows // CUTS
    steps = A * CUTS

    def a_of(i):
        return lax.rem(a_me + spread(i // CUTS, A), A)

    def core_copy(i, j):
        idx = i * B + j
        return pltpu.make_async_remote_copy(
            src_ref=p_send.at[idx], dst_ref=rc.at[idx],
            send_sem=c_send_sem, recv_sem=c_recv_sem.at[idx],
            device_id={"vocab": at(a_me, b_me, 1 - core)}, device_id_type=pl.DeviceIdType.MESH,
        )

    def b_copy(i, j):
        return pltpu.make_async_remote_copy(
            src_ref=sb.at[i * (B - 1) + j], dst_ref=rb.at[i * (B - 1) + j],
            send_sem=b_send_sem, recv_sem=b_recv_sem.at[i * (B - 1) + j],
            device_id={"vocab": at(a_me, lax.rem(b_me + 1 + j, B), core)}, device_id_type=pl.DeviceIdType.MESH,
        )

    def a_copy(i):
        return pltpu.make_async_remote_copy(
            src_ref=sa.at[i], dst_ref=ra.at[i],
            send_sem=a_send_sem, recv_sem=a_recv_sem.at[i],
            device_id={"vocab": at(a_of(i), b_me, core)}, device_id_type=pl.DeviceIdType.MESH,
        )

    def product(i, j, c):
        owner = at(a_of(i), lax.rem(b_me + 1 + j, B), c)
        start = pl.multiple_of(owner * rows + lax.rem(i, CUTS) * cut, cut)
        return jnp.dot(w_ref[pl.ds(start, cut), :], res_ref[...], preferred_element_type=jnp.float32)

    def step(i, carry):
        for j in range(B):
            p_send[i * B + j] = product(i, j, 1 - core)
            core_copy(i, j).start()
            if j >= 1:
                pass_on(i, j - 1)
            p_own[i * B + j] = product(i, j, core)
        return carry

    def pass_on(i, j):
        core_copy(i, j).wait_recv()
        encode(p_own[i * B + j] + rc[i * B + j], sb.at[i * (B - 1) + j])
        b_copy(i, j).start()

    def collected(i):
        core_copy(i, B - 1).wait_recv()
        acc = p_own[i * B + B - 1] + rc[i * B + B - 1]
        for j in range(B - 1):
            b_copy(i, j).wait_recv()
            acc += decode(rb.at[i * (B - 1) + j])
        return acc

    lax.fori_loop(0, steps, step, 0)
    for i in range(steps - CUTS):
        encode(collected(i), sa.at[i])
        a_copy(i).start()
    for s in range(CUTS):
        out_ref[s * cut:(s + 1) * cut, :] = collected(steps - CUTS + s)
    for i in range(steps - CUTS):
        part = (i % CUTS) * cut
        a_copy(i).wait_recv()
        out_ref[part:part + cut, :] += decode(ra.at[i])

    def drained(ref, sem):
        pltpu.make_async_copy(ref, ref, sem).wait()

    drained(send_ref.at[pl.ds(1, n - 1)], a2a_send_sem)
    for which, gathered in enumerate((tstat, sstat, mass)):
        drained(gathered.at[pl.ds(1, n - 1)], small_send_sem.at[which])
    drained(p_send, c_send_sem)
    drained(rb, b_send_sem)
    drained(ra, a_send_sem)


def per_device(
    n, hidden, student_weight, teacher_codes, teacher_exps, pair_tile, pair_dest, pair_block, pair_map
):
    A, B = grid_of(n)
    tokens, d_full = hidden.shape
    v_local = student_weight.shape[1]
    rows = d_full // n
    cut = rows // CUTS
    tiles = teacher_codes.shape[0] // BLK
    slot_rows = CAP * BLK + META
    f32, bf16 = jnp.float32, jnp.bfloat16
    vmem = pl.BlockSpec(memory_space=pltpu.VMEM)
    smem = pl.BlockSpec(memory_space=pltpu.SMEM)
    hbm = pl.BlockSpec(memory_space=pl.ANY)
    dma = pltpu.SemaphoreType.DMA
    return pl.pallas_call(
        functools.partial(kernel, n, A, B),
        out_shape=jax.ShapeDtypeStruct((rows, tokens), f32),
        in_specs=[smem, smem, smem, hbm, hbm, vmem, vmem, vmem],
        out_specs=vmem,
        scratch_shapes=[
            pltpu.VMEM((d_full, v_local), bf16),
            pltpu.VMEM((tokens, d_full), bf16),
            pltpu.VMEM((tiles, BLK, tokens), bf16),
            pltpu.VMEM((CAP * BLK, tokens), bf16),
            pltpu.VMEM((n, slot_rows, tokens), bf16),
            pltpu.VMEM((n, slot_rows, tokens), bf16),
            pltpu.VMEM((3, 8, tokens), f32),
            pltpu.VMEM((n, 8, tokens), f32),
            pltpu.VMEM((n, 8, tokens), f32),
            pltpu.VMEM((n, 8, tokens), f32),
            pltpu.VMEM((v_local, tokens), f32),
            pltpu.VMEM((v_local, tokens), f32),
            pltpu.VMEM((v_local, tokens), bf16),
            pltpu.VMEM((A * CUTS * B, cut, tokens), f32),
            pltpu.VMEM((A * CUTS * B, cut, tokens), f32),
            pltpu.VMEM((A * CUTS * B, cut, tokens), f32),
            pltpu.VMEM((A * CUTS * (B - 1), cut + SCALE_ROWS, tokens), jnp.int16),
            pltpu.VMEM(((A - 1) * CUTS, cut + SCALE_ROWS, tokens), jnp.int16),
            pltpu.VMEM((A * CUTS * (B - 1), cut + SCALE_ROWS, tokens), jnp.int16),
            pltpu.VMEM(((A - 1) * CUTS, cut + SCALE_ROWS, tokens), jnp.int16),
            dma((W_CHUNKS,)),
            dma,
            dma,
            dma((n,)),
            dma((3,)),
            dma((3,)),
            dma,
            dma((A * CUTS * B,)),
            dma,
            dma((A * CUTS * (B - 1),)),
            dma,
            dma(((A - 1) * CUTS,)),
        ],
        compiler_params=pltpu.CompilerParams(
            collective_id=0, has_side_effects=True, vmem_limit_bytes=56 * 1024 * 1024
        ),
    )(
        pair_tile, pair_dest.reshape(-1), pair_block,
        hidden, student_weight, teacher_codes, teacher_exps, pair_map,
    ).astype(bf16)


def solution(mesh):
    return jax.shard_map(
        functools.partial(per_device, mesh.shape["vocab"]),
        mesh=mesh,
        in_specs=(
            P("groups", None),
            P(None, "vocab"),
            P("vocab", "groups"),
            P("vocab", "groups"),
            P("vocab"),
            P("vocab", None),
            P("vocab"),
            P("vocab", None),
        ),
        out_specs=P("vocab", "groups"),
        check_vma=False,
    )
```

```python
import functools

import jax
import jax.numpy as jnp
from jax import lax
from jax.experimental import pallas as pl
from jax.experimental.pallas import tpu as pltpu
from jax.sharding import PartitionSpec as P

BLK = 128
CAP = 2
GROUP = 32
W_CHUNKS = 8
SCALE_ROWS = 16
CUTS = 1
TOP_CODE = 32000.0
TINY = 1e-30

smoothing = 0.05
loss_scale = 64.0


def grid_of(owners):
    chips = owners // 2
    b = 1
    while (2 * b) * (2 * b) <= chips:
        b *= 2
    return chips // b, b


def encode(values, ref):
    rows = values.shape[0]
    top = jnp.maximum(jnp.max(jnp.abs(values), axis=0, keepdims=True), TINY)
    level = jnp.ceil(8.0 * jnp.log2(top))
    step = TOP_CODE / jnp.exp2(level * 0.125)
    codes = jnp.round(values * step).astype(jnp.int32)
    ref[0:rows, :] = codes.astype(jnp.int16)
    levels = jnp.broadcast_to(level, (SCALE_ROWS, values.shape[1])).astype(jnp.int32)
    ref[rows:rows + SCALE_ROWS, :] = levels.astype(jnp.int16)


def decode(ref):
    rows = ref.shape[0] - SCALE_ROWS
    level = ref[rows:rows + SCALE_ROWS, :].astype(jnp.int32).astype(jnp.float32)[0:1, :]
    scale = jnp.exp2(level * 0.125) * (1.0 / TOP_CODE)
    return ref[0:rows, :].astype(jnp.int32).astype(jnp.float32) * scale


def kernel(
    n, A, B,
    tile_s, dest_s, block_s, hidden_hbm, w_hbm, codes_ref, exps_ref, map_ref, out_ref,
    w_ref, h_ref, tl_ref, probs_ref, send_ref, recv_ref, send_meta, recv_meta, stat_send, tstat, sstat, mass, logits_ref, mapped_ref,
    res_ref, p_send, p_own, rc, sb, sa, rb, ra,
    w_sem, h_sem, a2a_send_sem, a2a_recv_sem, meta_send_sem, meta_recv_sem, small_send_sem, small_recv_sem,
    c_send_sem, c_recv_sem, b_send_sem, b_recv_sem, a_send_sem, a_recv_sem,
):
    me = lax.axis_index("vocab")
    pairs = dest_s.shape[0]
    v_local = w_ref.shape[1]
    d_full = w_ref.shape[0]
    rows = d_full // n
    tokens = h_ref.shape[0]
    tiles = tl_ref.shape[0]
    payload = CAP * BLK
    core = lax.rem(me, 2)
    chip = me // 2
    b_me = lax.rem(chip, B)
    a_me = chip // B

    def at(a, b, c):
        return (a * B + b) * 2 + c

    barrier = pltpu.get_barrier_semaphore()

    def greet(off, carry):
        pl.semaphore_signal(barrier, inc=1, device_id={"vocab": lax.rem(me + off, n)}, device_id_type=pl.DeviceIdType.MESH)
        return carry

    lax.fori_loop(1, n, greet, 0)

    h_copy = pltpu.make_async_copy(hidden_hbm, h_ref, h_sem)
    h_copy.start()
    w_rows = d_full // W_CHUNKS
    w_copies = []
    for c in range(W_CHUNKS):
        part = pl.ds(c * w_rows, w_rows)
        w_copies.append(pltpu.make_async_copy(w_hbm.at[part, :], w_ref.at[part, :], w_sem.at[c]))
        w_copies[-1].start()

    exps = exps_ref[...]
    scales = jnp.where(exps >= 1, 2.0, jnp.where(exps == 0, 1.0, jnp.where(exps == -1, 0.5, 0.25)))
    per_tile = BLK // GROUP
    peak = jnp.full((1, tokens), -jnp.inf, jnp.float32)
    for t in range(tiles):
        codes = codes_ref[t * BLK:(t + 1) * BLK, :].astype(jnp.float32)
        scale = scales[t * per_tile:(t + 1) * per_tile, :]
        values = (codes.reshape(per_tile, GROUP, tokens) * scale[:, None, :]).reshape(BLK, tokens)
        tl_ref[t] = values.astype(jnp.bfloat16)
        peak = jnp.maximum(peak, jnp.max(values, axis=0, keepdims=True))
    total = jnp.zeros((1, tokens), jnp.float32)
    for t in range(tiles):
        total += jnp.sum(jnp.exp(tl_ref[t].astype(jnp.float32) - peak), axis=0, keepdims=True)

    row8 = lax.broadcasted_iota(jnp.int32, (8, tokens), 0)

    def small_copy(which, gathered, off):
        return pltpu.make_async_remote_copy(
            src_ref=stat_send.at[which],
            dst_ref=gathered.at[off],
            send_sem=small_send_sem.at[which],
            recv_sem=small_recv_sem.at[which],
            device_id={"vocab": lax.rem(me + off, n)},
            device_id_type=pl.DeviceIdType.MESH,
        )

    def share(which, gathered, tile):
        stat_send[which] = tile
        gathered[0] = tile

        def one(off, carry):
            small_copy(which, gathered, off).start()
            return carry

        lax.fori_loop(1, n, one, 0)

    def collect(which, gathered):
        others = gathered.at[pl.ds(1, n - 1)]
        pltpu.make_async_copy(others, others, small_recv_sem.at[which]).wait()

    def normalizer(gathered):
        peaks = gathered[:, 0, :]
        totals = gathered[:, 1, :]
        top = jnp.max(peaks, axis=0, keepdims=True)
        return top + jnp.log(jnp.sum(totals * jnp.exp(peaks - top), axis=0, keepdims=True))

    pl.semaphore_wait(barrier, n - 1)
    share(0, tstat, jnp.where(row8 == 0, peak, total))


    def fill(off, ref, meta):
        target = lax.rem(me + off, n)

        def look(k, found):
            first, second = found
            hit = dest_s[k] == target
            second = jnp.where(hit & (first >= 0), k, second)
            first = jnp.where(hit & (first < 0), k, first)
            return first, second

        first, second = lax.fori_loop(0, pairs, look, (jnp.int32(-1), jnp.int32(-1)), unroll=8)
        for slot, source in enumerate((first, second)):
            index = jnp.maximum(source, 0)
            ref[off, slot * BLK:(slot + 1) * BLK, :] = tl_ref[tile_s[index]]
            entries = map_ref[pl.ds(index, 1), :]
            places = jnp.where(entries < BLK, block_s[index] * BLK + entries, v_local)
            meta[off, slot:slot + 1, :] = jnp.where(source >= 0, places, v_local)

    def slot_copy(off):
        return pltpu.make_async_remote_copy(
            src_ref=send_ref.at[off],
            dst_ref=recv_ref.at[off],
            send_sem=a2a_send_sem,
            recv_sem=a2a_recv_sem.at[off],
            device_id={"vocab": lax.rem(me + off, n)},
            device_id_type=pl.DeviceIdType.MESH,
        )

    def spread(i, size):
        odd = lax.rem(i, 2)
        return size // 2 + odd * ((i + 1) // 2) - (1 - odd) * (i // 2)

    def slot_order(i):
        odd = lax.rem(i, 2)
        return spread(odd * (n - 2 - i // 2) + (1 - odd) * (i // 2), n)

    def meta_copy(off):
        return pltpu.make_async_remote_copy(
            src_ref=send_meta.at[off],
            dst_ref=recv_meta.at[off],
            send_sem=meta_send_sem,
            recv_sem=meta_recv_sem.at[off],
            device_id={"vocab": lax.rem(me + off, n)},
            device_id_type=pl.DeviceIdType.MESH,
        )

    def send_slot(i, carry):
        off = slot_order(i)
        fill(off, send_ref, send_meta)
        slot_copy(off).start()
        meta_copy(off).start()
        return carry

    early = n // 3
    lax.fori_loop(0, early, send_slot, 0)

    h_copy.wait()
    logits = jnp.zeros((tokens, v_local), jnp.float32)
    for c in range(W_CHUNKS):
        w_copies[c].wait()
        logits += jnp.dot(
            h_ref[:, c * w_rows:(c + 1) * w_rows],
            w_ref[c * w_rows:(c + 1) * w_rows, :],
            preferred_element_type=jnp.float32,
        )
    logits = logits.T
    logits_ref[...] = logits
    s_peak = jnp.max(logits, axis=0, keepdims=True)
    s_total = jnp.sum(jnp.exp(logits - s_peak), axis=0, keepdims=True)
    share(1, sstat, jnp.where(row8 == 0, s_peak, s_total))

    collect(0, tstat)
    lse = normalizer(tstat)
    tile_row = lax.broadcasted_iota(jnp.int32, (tiles, BLK), 0)

    def count(k, counts):
        valid = jnp.where(map_ref[pl.ds(k, 1), :] < BLK, 1.0, 0.0)
        return counts + jnp.where(tile_row == tile_s[k], valid, 0.0)

    counts = lax.fori_loop(0, pairs, count, jnp.zeros((tiles, BLK), jnp.float32))
    counts = counts.astype(jnp.bfloat16)
    part_mass = jnp.zeros((tiles, tokens), jnp.float32)
    for t in range(tiles):
        probs = jnp.exp(tl_ref[t].astype(jnp.float32) - lse).astype(jnp.bfloat16)
        term = jnp.dot(counts, probs, preferred_element_type=jnp.float32)
        part_mass += jnp.where(lax.broadcasted_iota(jnp.int32, (tiles, tokens), 0) == t, term, 0.0)
    part_mass = jnp.sum(part_mass, axis=0, keepdims=True)
    share(2, mass, jnp.broadcast_to(part_mass, (8, tokens)))

    lax.fori_loop(early, n - 1, send_slot, 0)
    fill(0, recv_ref, recv_meta)

    mapped_ref[...] = jnp.zeros_like(mapped_ref)
    entry = lax.broadcasted_iota(jnp.int32, (v_local, BLK), 0)

    def join(off):
        probs_ref[...] = jnp.exp(recv_ref[off, 0:payload, :].astype(jnp.float32) - lse).astype(jnp.bfloat16)
        pickers = []
        for slot in range(CAP):
            places = recv_meta[off, slot:slot + 1, :]
            pickers.append(jnp.where(entry == places, 1.0, 0.0).astype(jnp.bfloat16))
        picker = jnp.concatenate(pickers, axis=1)
        mapped_ref[...] += jnp.dot(picker, probs_ref[...], preferred_element_type=jnp.float32)

    join(0)

    def join_next(i, carry):
        off = slot_order(i)
        slot_copy(off).wait_recv()
        meta_copy(off).wait_recv()
        join(off)
        return carry

    lax.fori_loop(0, n - 1, join_next, 0)

    collect(1, sstat)
    collect(2, mass)
    s_lse = normalizer(sstat)
    mass_total = jnp.sum(mass[:, 0, :], axis=0, keepdims=True)
    target = (mapped_ref[...] + smoothing / (v_local * n)) / (mass_total + smoothing)
    s_probs = jnp.exp(logits_ref[...] - s_lse)
    res_ref[...] = (loss_scale * (s_probs - target)).astype(jnp.bfloat16)

    cut = rows // CUTS
    steps = A * CUTS

    def a_of(i):
        return lax.rem(a_me + spread(i // CUTS, A), A)

    def core_copy(i, j):
        idx = i * B + j
        return pltpu.make_async_remote_copy(
            src_ref=p_send.at[idx], dst_ref=rc.at[idx],
            send_sem=c_send_sem, recv_sem=c_recv_sem.at[idx],
            device_id={"vocab": at(a_me, b_me, 1 - core)}, device_id_type=pl.DeviceIdType.MESH,
        )

    def b_copy(i, j):
        return pltpu.make_async_remote_copy(
            src_ref=sb.at[i * (B - 1) + j], dst_ref=rb.at[i * (B - 1) + j],
            send_sem=b_send_sem, recv_sem=b_recv_sem.at[i * (B - 1) + j],
            device_id={"vocab": at(a_me, lax.rem(b_me + 1 + j, B), core)}, device_id_type=pl.DeviceIdType.MESH,
        )

    def a_copy(i):
        return pltpu.make_async_remote_copy(
            src_ref=sa.at[i], dst_ref=ra.at[i],
            send_sem=a_send_sem, recv_sem=a_recv_sem.at[i],
            device_id={"vocab": at(a_of(i), b_me, core)}, device_id_type=pl.DeviceIdType.MESH,
        )

    def product(i, j, c):
        owner = at(a_of(i), lax.rem(b_me + 1 + j, B), c)
        start = pl.multiple_of(owner * rows + lax.rem(i, CUTS) * cut, cut)
        return jnp.dot(w_ref[pl.ds(start, cut), :], res_ref[...], preferred_element_type=jnp.float32)

    def step(i, carry):
        for j in range(B):
            p_send[i * B + j] = product(i, j, 1 - core)
            core_copy(i, j).start()
            if j >= 1:
                pass_on(i, j - 1)
            p_own[i * B + j] = product(i, j, core)
        return carry

    def pass_on(i, j):
        core_copy(i, j).wait_recv()
        encode(p_own[i * B + j] + rc[i * B + j], sb.at[i * (B - 1) + j])
        b_copy(i, j).start()

    def collected(i):
        core_copy(i, B - 1).wait_recv()
        acc = p_own[i * B + B - 1] + rc[i * B + B - 1]
        for j in range(B - 1):
            b_copy(i, j).wait_recv()
            acc += decode(rb.at[i * (B - 1) + j])
        return acc

    lax.fori_loop(0, steps, step, 0)
    for i in range(steps - CUTS):
        encode(collected(i), sa.at[i])
        a_copy(i).start()
    for s in range(CUTS):
        out_ref[s * cut:(s + 1) * cut, :] = collected(steps - CUTS + s)
    for i in range(steps - CUTS):
        part = (i % CUTS) * cut
        a_copy(i).wait_recv()
        out_ref[part:part + cut, :] += decode(ra.at[i])

    def drained(ref, sem):
        pltpu.make_async_copy(ref, ref, sem).wait()

    drained(send_ref.at[pl.ds(1, n - 1)], a2a_send_sem)
    drained(send_meta.at[pl.ds(1, n - 1)], meta_send_sem)
    for which, gathered in enumerate((tstat, sstat, mass)):
        drained(gathered.at[pl.ds(1, n - 1)], small_send_sem.at[which])
    drained(p_send, c_send_sem)
    drained(rb, b_send_sem)
    drained(ra, a_send_sem)


def per_device(
    n, hidden, student_weight, teacher_codes, teacher_exps, pair_tile, pair_dest, pair_block, pair_map
):
    A, B = grid_of(n)
    tokens, d_full = hidden.shape
    v_local = student_weight.shape[1]
    rows = d_full // n
    cut = rows // CUTS
    tiles = teacher_codes.shape[0] // BLK
    slot_rows = CAP * BLK
    f32, bf16 = jnp.float32, jnp.bfloat16
    vmem = pl.BlockSpec(memory_space=pltpu.VMEM)
    smem = pl.BlockSpec(memory_space=pltpu.SMEM)
    hbm = pl.BlockSpec(memory_space=pl.ANY)
    dma = pltpu.SemaphoreType.DMA
    return pl.pallas_call(
        functools.partial(kernel, n, A, B),
        out_shape=jax.ShapeDtypeStruct((rows, tokens), f32),
        in_specs=[smem, smem, smem, hbm, hbm, vmem, vmem, vmem],
        out_specs=vmem,
        scratch_shapes=[
            pltpu.VMEM((d_full, v_local), bf16),
            pltpu.VMEM((tokens, d_full), bf16),
            pltpu.VMEM((tiles, BLK, tokens), bf16),
            pltpu.VMEM((CAP * BLK, tokens), bf16),
            pltpu.VMEM((n, slot_rows, tokens), bf16),
            pltpu.VMEM((n, slot_rows, tokens), bf16),
            pltpu.VMEM((n, CAP, BLK), jnp.int32),
            pltpu.VMEM((n, CAP, BLK), jnp.int32),
            pltpu.VMEM((3, 8, tokens), f32),
            pltpu.VMEM((n, 8, tokens), f32),
            pltpu.VMEM((n, 8, tokens), f32),
            pltpu.VMEM((n, 8, tokens), f32),
            pltpu.VMEM((v_local, tokens), f32),
            pltpu.VMEM((v_local, tokens), f32),
            pltpu.VMEM((v_local, tokens), bf16),
            pltpu.VMEM((A * CUTS * B, cut, tokens), f32),
            pltpu.VMEM((A * CUTS * B, cut, tokens), f32),
            pltpu.VMEM((A * CUTS * B, cut, tokens), f32),
            pltpu.VMEM((A * CUTS * (B - 1), cut + SCALE_ROWS, tokens), jnp.int16),
            pltpu.VMEM(((A - 1) * CUTS, cut + SCALE_ROWS, tokens), jnp.int16),
            pltpu.VMEM((A * CUTS * (B - 1), cut + SCALE_ROWS, tokens), jnp.int16),
            pltpu.VMEM(((A - 1) * CUTS, cut + SCALE_ROWS, tokens), jnp.int16),
            dma((W_CHUNKS,)),
            dma,
            dma,
            dma((n,)),
            dma,
            dma((n,)),
            dma((3,)),
            dma((3,)),
            dma,
            dma((A * CUTS * B,)),
            dma,
            dma((A * CUTS * (B - 1),)),
            dma,
            dma(((A - 1) * CUTS,)),
        ],
        compiler_params=pltpu.CompilerParams(
            collective_id=0, has_side_effects=True, vmem_limit_bytes=56 * 1024 * 1024
        ),
    )(
        pair_tile, pair_dest.reshape(-1), pair_block,
        hidden, student_weight, teacher_codes, teacher_exps, pair_map,
    ).astype(bf16)


def solution(mesh):
    return jax.shard_map(
        functools.partial(per_device, mesh.shape["vocab"]),
        mesh=mesh,
        in_specs=(
            P("groups", None),
            P(None, "vocab"),
            P("vocab", "groups"),
            P("vocab", "groups"),
            P("vocab"),
            P("vocab", None),
            P("vocab"),
            P("vocab", None),
        ),
        out_specs=P("vocab", "groups"),
        check_vma=False,
    )
```

```python
import functools

import jax
import jax.numpy as jnp
from jax import lax
from jax.experimental import pallas as pl
from jax.experimental.pallas import tpu as pltpu
from jax.sharding import PartitionSpec as P

BLK = 128
CAP = 2
GROUP = 32
W_CHUNKS = 8
SCALE_ROWS = 16
CUTS = 1
TOP_CODE = 32000.0
TINY = 1e-30

smoothing = 0.05
loss_scale = 64.0


def grid_of(owners):
    chips = owners // 2
    b = 1
    while (2 * b) * (2 * b) <= chips:
        b *= 2
    return chips // b, b


def encode(values, ref):
    rows = values.shape[0]
    top = jnp.maximum(jnp.max(jnp.abs(values), axis=0, keepdims=True), TINY)
    level = jnp.ceil(8.0 * jnp.log2(top))
    step = TOP_CODE * jnp.exp2(level * -0.125)
    codes = jnp.round(values * step).astype(jnp.int32)
    ref[0:rows, :] = codes.astype(jnp.int16)
    levels = jnp.broadcast_to(level, (SCALE_ROWS, values.shape[1])).astype(jnp.int32)
    ref[rows:rows + SCALE_ROWS, :] = levels.astype(jnp.int16)


def decode(ref):
    rows = ref.shape[0] - SCALE_ROWS
    level = ref[rows:rows + SCALE_ROWS, :].astype(jnp.int32).astype(jnp.float32)[0:1, :]
    scale = jnp.exp2(level * 0.125) * (1.0 / TOP_CODE)
    return ref[0:rows, :].astype(jnp.int32).astype(jnp.float32) * scale


def kernel(
    n, A, B,
    tile_s, dest_s, block_s, hidden_hbm, w_hbm, codes_ref, exps_ref, map_ref, out_ref,
    w_ref, h_ref, tl_ref, probs_ref, send_ref, recv_ref, send_meta, recv_meta, stat_send, tstat, sstat, mass, logits_ref, mapped_ref,
    res_ref, p_send, p_own, rc, sb, sa, rb, ra,
    w_sem, h_sem, a2a_send_sem, a2a_recv_sem, meta_send_sem, meta_recv_sem, small_send_sem, small_recv_sem,
    c_send_sem, c_recv_sem, b_send_sem, b_recv_sem, a_send_sem, a_recv_sem,
):
    me = lax.axis_index("vocab")
    pairs = dest_s.shape[0]
    v_local = w_ref.shape[1]
    d_full = w_ref.shape[0]
    rows = d_full // n
    tokens = h_ref.shape[0]
    tiles = tl_ref.shape[0]
    payload = CAP * BLK
    core = lax.rem(me, 2)
    chip = me // 2
    b_me = lax.rem(chip, B)
    a_me = chip // B

    def at(a, b, c):
        return (a * B + b) * 2 + c

    barrier = pltpu.get_barrier_semaphore()

    def greet(off, carry):
        pl.semaphore_signal(barrier, inc=1, device_id={"vocab": lax.rem(me + off, n)}, device_id_type=pl.DeviceIdType.MESH)
        return carry

    lax.fori_loop(1, n, greet, 0)

    h_copy = pltpu.make_async_copy(hidden_hbm, h_ref, h_sem)
    h_copy.start()
    w_rows = d_full // W_CHUNKS
    w_copies = []
    for c in range(W_CHUNKS):
        part = pl.ds(c * w_rows, w_rows)
        w_copies.append(pltpu.make_async_copy(w_hbm.at[part, :], w_ref.at[part, :], w_sem.at[c]))
        w_copies[-1].start()

    exps = exps_ref[...]
    scales = jnp.where(exps >= 1, 2.0, jnp.where(exps == 0, 1.0, jnp.where(exps == -1, 0.5, 0.25)))
    per_tile = BLK // GROUP
    peak = jnp.full((1, tokens), -jnp.inf, jnp.float32)
    for t in range(tiles):
        codes = codes_ref[t * BLK:(t + 1) * BLK, :].astype(jnp.float32)
        scale = scales[t * per_tile:(t + 1) * per_tile, :]
        values = (codes.reshape(per_tile, GROUP, tokens) * scale[:, None, :]).reshape(BLK, tokens)
        tl_ref[t] = values.astype(jnp.bfloat16)
        peak = jnp.maximum(peak, jnp.max(values, axis=0, keepdims=True))
    total = jnp.zeros((1, tokens), jnp.float32)
    for t in range(tiles):
        total += jnp.sum(jnp.exp(tl_ref[t].astype(jnp.float32) - peak), axis=0, keepdims=True)

    row8 = lax.broadcasted_iota(jnp.int32, (8, tokens), 0)

    def small_copy(which, gathered, off):
        return pltpu.make_async_remote_copy(
            src_ref=stat_send.at[which],
            dst_ref=gathered.at[off],
            send_sem=small_send_sem.at[which],
            recv_sem=small_recv_sem.at[which],
            device_id={"vocab": lax.rem(me + off, n)},
            device_id_type=pl.DeviceIdType.MESH,
        )

    def share(which, gathered, tile):
        stat_send[which] = tile
        gathered[0] = tile

        def one(off, carry):
            small_copy(which, gathered, off).start()
            return carry

        lax.fori_loop(1, n, one, 0)

    def collect(which, gathered):
        others = gathered.at[pl.ds(1, n - 1)]
        pltpu.make_async_copy(others, others, small_recv_sem.at[which]).wait()

    def normalizer(gathered):
        peaks = gathered[:, 0, :]
        totals = gathered[:, 1, :]
        top = jnp.max(peaks, axis=0, keepdims=True)
        return top + jnp.log(jnp.sum(totals * jnp.exp(peaks - top), axis=0, keepdims=True))

    pl.semaphore_wait(barrier, n - 1)
    share(0, tstat, jnp.where(row8 == 0, peak, total))


    def fill(off, ref, meta):
        target = lax.rem(me + off, n)

        def look(k, found):
            first, second = found
            hit = dest_s[k] == target
            second = jnp.where(hit & (first >= 0), k, second)
            first = jnp.where(hit & (first < 0), k, first)
            return first, second

        first, second = lax.fori_loop(0, pairs, look, (jnp.int32(-1), jnp.int32(-1)), unroll=8)
        for slot, source in enumerate((first, second)):
            index = jnp.maximum(source, 0)
            ref[off, slot * BLK:(slot + 1) * BLK, :] = tl_ref[tile_s[index]]
            entries = map_ref[pl.ds(index, 1), :]
            places = jnp.where(entries < BLK, block_s[index] * BLK + entries, v_local)
            meta[off, slot:slot + 1, :] = jnp.where(source >= 0, places, v_local)

    def slot_copy(off):
        return pltpu.make_async_remote_copy(
            src_ref=send_ref.at[off],
            dst_ref=recv_ref.at[off],
            send_sem=a2a_send_sem,
            recv_sem=a2a_recv_sem.at[off],
            device_id={"vocab": lax.rem(me + off, n)},
            device_id_type=pl.DeviceIdType.MESH,
        )

    def spread(i, size):
        odd = lax.rem(i, 2)
        return size // 2 + odd * ((i + 1) // 2) - (1 - odd) * (i // 2)

    def slot_order(i):
        odd = lax.rem(i, 2)
        return spread(odd * (n - 2 - i // 2) + (1 - odd) * (i // 2), n)

    def meta_copy(off):
        return pltpu.make_async_remote_copy(
            src_ref=send_meta.at[off],
            dst_ref=recv_meta.at[off],
            send_sem=meta_send_sem,
            recv_sem=meta_recv_sem.at[off],
            device_id={"vocab": lax.rem(me + off, n)},
            device_id_type=pl.DeviceIdType.MESH,
        )

    def send_slot(i, carry):
        off = slot_order(i)
        fill(off, send_ref, send_meta)
        slot_copy(off).start()
        meta_copy(off).start()
        return carry

    early = n // 3
    lax.fori_loop(0, early, send_slot, 0)

    h_copy.wait()
    logits = jnp.zeros((tokens, v_local), jnp.float32)
    for c in range(W_CHUNKS):
        w_copies[c].wait()
        logits += jnp.dot(
            h_ref[:, c * w_rows:(c + 1) * w_rows],
            w_ref[c * w_rows:(c + 1) * w_rows, :],
            preferred_element_type=jnp.float32,
        )
    logits = logits.T
    logits_ref[...] = logits
    s_peak = jnp.max(logits, axis=0, keepdims=True)
    s_total = jnp.sum(jnp.exp(logits - s_peak), axis=0, keepdims=True)
    share(1, sstat, jnp.where(row8 == 0, s_peak, s_total))

    collect(0, tstat)
    lse = normalizer(tstat)
    tile_row = lax.broadcasted_iota(jnp.int32, (tiles, BLK), 0)

    def count(k, counts):
        valid = jnp.where(map_ref[pl.ds(k, 1), :] < BLK, 1.0, 0.0)
        return counts + jnp.where(tile_row == tile_s[k], valid, 0.0)

    counts = lax.fori_loop(0, pairs, count, jnp.zeros((tiles, BLK), jnp.float32))
    counts = counts.astype(jnp.bfloat16)
    part_mass = jnp.zeros((tiles, tokens), jnp.float32)
    for t in range(tiles):
        probs = jnp.exp(tl_ref[t].astype(jnp.float32) - lse).astype(jnp.bfloat16)
        term = jnp.dot(counts, probs, preferred_element_type=jnp.float32)
        part_mass += jnp.where(lax.broadcasted_iota(jnp.int32, (tiles, tokens), 0) == t, term, 0.0)
    part_mass = jnp.sum(part_mass, axis=0, keepdims=True)
    share(2, mass, jnp.broadcast_to(part_mass, (8, tokens)))

    lax.fori_loop(early, n - 1, send_slot, 0)
    fill(0, recv_ref, recv_meta)

    mapped_ref[...] = jnp.zeros_like(mapped_ref)
    entry = lax.broadcasted_iota(jnp.int32, (v_local, BLK), 0)

    def join(off):
        probs_ref[...] = jnp.exp(recv_ref[off, 0:payload, :].astype(jnp.float32) - lse).astype(jnp.bfloat16)
        pickers = []
        for slot in range(CAP):
            places = recv_meta[off, slot:slot + 1, :]
            pickers.append(jnp.where(entry == places, 1.0, 0.0).astype(jnp.bfloat16))
        picker = jnp.concatenate(pickers, axis=1)
        mapped_ref[...] += jnp.dot(picker, probs_ref[...], preferred_element_type=jnp.float32)

    join(0)

    def join_next(i, carry):
        off = slot_order(i)
        slot_copy(off).wait_recv()
        meta_copy(off).wait_recv()
        join(off)
        return carry

    lax.fori_loop(0, n - 1, join_next, 0)

    collect(1, sstat)
    collect(2, mass)
    s_lse = normalizer(sstat)
    mass_total = jnp.sum(mass[:, 0, :], axis=0, keepdims=True)
    target = (mapped_ref[...] + smoothing / (v_local * n)) / (mass_total + smoothing)
    s_probs = jnp.exp(logits_ref[...] - s_lse)
    res_ref[...] = (loss_scale * (s_probs - target)).astype(jnp.bfloat16)

    cut = rows // CUTS
    steps = A * CUTS

    def a_of(i):
        return lax.rem(a_me + spread(i // CUTS, A), A)

    def core_copy(i, j):
        idx = i * B + j
        return pltpu.make_async_remote_copy(
            src_ref=p_send.at[idx], dst_ref=rc.at[idx],
            send_sem=c_send_sem, recv_sem=c_recv_sem.at[idx],
            device_id={"vocab": at(a_me, b_me, 1 - core)}, device_id_type=pl.DeviceIdType.MESH,
        )

    def b_copy(i, j):
        return pltpu.make_async_remote_copy(
            src_ref=sb.at[i * (B - 1) + j], dst_ref=rb.at[i * (B - 1) + j],
            send_sem=b_send_sem, recv_sem=b_recv_sem.at[i * (B - 1) + j],
            device_id={"vocab": at(a_me, lax.rem(b_me + 1 + j, B), core)}, device_id_type=pl.DeviceIdType.MESH,
        )

    def a_copy(i):
        return pltpu.make_async_remote_copy(
            src_ref=sa.at[i], dst_ref=ra.at[i],
            send_sem=a_send_sem, recv_sem=a_recv_sem.at[i],
            device_id={"vocab": at(a_of(i), b_me, core)}, device_id_type=pl.DeviceIdType.MESH,
        )

    def product(i, j, c):
        owner = at(a_of(i), lax.rem(b_me + 1 + j, B), c)
        start = pl.multiple_of(owner * rows + lax.rem(i, CUTS) * cut, cut)
        return jnp.dot(w_ref[pl.ds(start, cut), :], res_ref[...], preferred_element_type=jnp.float32)

    def step(i, carry):
        for j in range(B):
            encode(product(i, j, 1 - core), p_send.at[i * B + j])
            core_copy(i, j).start()
            if j >= 1:
                pass_on(i, j - 1)
            p_own[i * B + j] = product(i, j, core)
        return carry

    def pass_on(i, j):
        core_copy(i, j).wait_recv()
        encode(p_own[i * B + j] + decode(rc.at[i * B + j]), sb.at[i * (B - 1) + j])
        b_copy(i, j).start()

    def collected(i):
        core_copy(i, B - 1).wait_recv()
        acc = p_own[i * B + B - 1] + decode(rc.at[i * B + B - 1])
        for j in range(B - 1):
            b_copy(i, j).wait_recv()
            acc += decode(rb.at[i * (B - 1) + j])
        return acc

    lax.fori_loop(0, steps, step, 0)
    for i in range(steps - CUTS):
        encode(collected(i), sa.at[i])
        a_copy(i).start()
    for s in range(CUTS):
        out_ref[s * cut:(s + 1) * cut, :] = collected(steps - CUTS + s)
    for i in range(steps - CUTS):
        part = (i % CUTS) * cut
        a_copy(i).wait_recv()
        out_ref[part:part + cut, :] += decode(ra.at[i])

    def drained(ref, sem):
        pltpu.make_async_copy(ref, ref, sem).wait()

    drained(send_ref.at[pl.ds(1, n - 1)], a2a_send_sem)
    drained(send_meta.at[pl.ds(1, n - 1)], meta_send_sem)
    for which, gathered in enumerate((tstat, sstat, mass)):
        drained(gathered.at[pl.ds(1, n - 1)], small_send_sem.at[which])
    drained(p_send, c_send_sem)
    drained(rb, b_send_sem)
    drained(ra, a_send_sem)


def per_device(
    n, hidden, student_weight, teacher_codes, teacher_exps, pair_tile, pair_dest, pair_block, pair_map
):
    A, B = grid_of(n)
    tokens, d_full = hidden.shape
    v_local = student_weight.shape[1]
    rows = d_full // n
    cut = rows // CUTS
    tiles = teacher_codes.shape[0] // BLK
    slot_rows = CAP * BLK
    f32, bf16 = jnp.float32, jnp.bfloat16
    vmem = pl.BlockSpec(memory_space=pltpu.VMEM)
    smem = pl.BlockSpec(memory_space=pltpu.SMEM)
    hbm = pl.BlockSpec(memory_space=pl.ANY)
    dma = pltpu.SemaphoreType.DMA
    return pl.pallas_call(
        functools.partial(kernel, n, A, B),
        out_shape=jax.ShapeDtypeStruct((rows, tokens), f32),
        in_specs=[smem, smem, smem, hbm, hbm, vmem, vmem, vmem],
        out_specs=vmem,
        scratch_shapes=[
            pltpu.VMEM((d_full, v_local), bf16),
            pltpu.VMEM((tokens, d_full), bf16),
            pltpu.VMEM((tiles, BLK, tokens), bf16),
            pltpu.VMEM((CAP * BLK, tokens), bf16),
            pltpu.VMEM((n, slot_rows, tokens), bf16),
            pltpu.VMEM((n, slot_rows, tokens), bf16),
            pltpu.VMEM((n, CAP, BLK), jnp.int32),
            pltpu.VMEM((n, CAP, BLK), jnp.int32),
            pltpu.VMEM((3, 8, tokens), f32),
            pltpu.VMEM((n, 8, tokens), f32),
            pltpu.VMEM((n, 8, tokens), f32),
            pltpu.VMEM((n, 8, tokens), f32),
            pltpu.VMEM((v_local, tokens), f32),
            pltpu.VMEM((v_local, tokens), f32),
            pltpu.VMEM((v_local, tokens), bf16),
            pltpu.VMEM((A * CUTS * B, cut + SCALE_ROWS, tokens), jnp.int16),
            pltpu.VMEM((A * CUTS * B, cut, tokens), f32),
            pltpu.VMEM((A * CUTS * B, cut + SCALE_ROWS, tokens), jnp.int16),
            pltpu.VMEM((A * CUTS * (B - 1), cut + SCALE_ROWS, tokens), jnp.int16),
            pltpu.VMEM(((A - 1) * CUTS, cut + SCALE_ROWS, tokens), jnp.int16),
            pltpu.VMEM((A * CUTS * (B - 1), cut + SCALE_ROWS, tokens), jnp.int16),
            pltpu.VMEM(((A - 1) * CUTS, cut + SCALE_ROWS, tokens), jnp.int16),
            dma((W_CHUNKS,)),
            dma,
            dma,
            dma((n,)),
            dma,
            dma((n,)),
            dma((3,)),
            dma((3,)),
            dma,
            dma((A * CUTS * B,)),
            dma,
            dma((A * CUTS * (B - 1),)),
            dma,
            dma(((A - 1) * CUTS,)),
        ],
        compiler_params=pltpu.CompilerParams(
            collective_id=0, has_side_effects=True, vmem_limit_bytes=56 * 1024 * 1024
        ),
    )(
        pair_tile, pair_dest.reshape(-1), pair_block,
        hidden, student_weight, teacher_codes, teacher_exps, pair_map,
    ).astype(bf16)


def solution(mesh):
    return jax.shard_map(
        functools.partial(per_device, mesh.shape["vocab"]),
        mesh=mesh,
        in_specs=(
            P("groups", None),
            P(None, "vocab"),
            P("vocab", "groups"),
            P("vocab", "groups"),
            P("vocab"),
            P("vocab", None),
            P("vocab"),
            P("vocab", None),
        ),
        out_specs=P("vocab", "groups"),
        check_vma=False,
    )
```
